32 devices in a mesh: dom: 8 (over z, y), node: 4 (over x, core).
Axes of the slice: x: 2, y: 2, z: 4, core: 2. Of those that a mesh axis runs over, the one named last changes fastest.
Arguments:
- positions: float32 [3, 65536], P(None, ('dom', 'node')), may hold values from -6 to 6
- masses: float32 [65536], P(('dom', 'node')), may hold values from 0.5 to 2
- metric: float32 [6, 65536], P(None, ('dom', 'node')), may hold values from -0.75 to 2.5, as said below
- energy: float32 [65536], P(('dom', 'node')), may hold values from 0.5 to 2
- local_pairs: int32 [512, 1], P(('dom', 'node')), may hold values from 0 to 15
- ghost_pairs: int32 [32, 32], P(('dom', 'node')), may hold values from 0 to 31, each once within a row
- node_sends: int32 [32, 4, 2], P(('dom', 'node')), may hold values from 0 to 15, as said below
- domain_sends: int32 [32, 2, 12], P(('dom', 'node')), may hold values from 0 to 15, as said below
Outputs:
- final_metric: float32 [6, 65536], P(None, ('dom', 'node'))
- density: float32 [65536], P(('dom', 'node'))
- acceleration: float32 [3, 65536], P(None, ('dom', 'node'))
The draws below stay inside these ranges and needn't reach their ends.
Inputs may be any that keep to these rules, and one draw needn't show every extreme that they name: `local_pairs`: indices of blocks within the owning device. `ghost_pairs`: each device's row names each of its 32 ghost slots exactly once. `node_sends`: indices of blocks within the sending device; each device sends exactly 2 blocks to each device of its node group, itself included, all 8 of them different blocks. `domain_sends`: indices of blocks within the sending device; row 0 goes to the previous domain, row 1 to the next, exactly 12 different blocks in each row. `metric`: each particle's six numbers form a positive definite symmetric matrix.
All inputs are finite; a program needn't handle non-finite values.
Results may differ from the reference program's by a relative error of at most 0.0001.
Values sent between devices are 32-bit elements; how exact they have to be, the bound alone decides.
A program may use at most 64 MiB of HBM per device.

```python
import math
import jax
import jax.numpy as jnp
from jax import lax

NB = 16
P_SIZE = 128
KL = 1
KG = 2
ITERS = 3
CAPN = 2
DEVS = 32
BLOCKS = 512
PARTICLES = 65536
GHOSTS = 32
CAPD = 12
N_DOM = 8
N_NODE = 4


def draw_metric(key, part):
    key = jax.random.fold_in(key, 11)
    keys = jax.random.split(key, 2)
    diagonal = jnp.exp(jax.random.uniform(keys[0], (3, PARTICLES), jnp.float32, math.log(0.4), math.log(2.5)))
    correlation = jax.random.uniform(keys[1], (3, PARTICLES), jnp.float32, -0.3, 0.3)
    scales = jnp.sqrt(diagonal)
    crossed = jnp.stack([correlation[0] * scales[0] * scales[1], correlation[1] * scales[0] * scales[2], correlation[2] * scales[1] * scales[2]])
    return jnp.concatenate([diagonal, crossed], axis=0).astype(jnp.float32)


def distinct_prefix(key, rows, count):
    keys = jax.random.split(key, rows)
    return jax.vmap(lambda single: jax.random.permutation(single, NB)[:count])(keys).astype(jnp.int32)


def draw_node_sends(key, part):
    key = jax.random.fold_in(key, 31)
    chosen = distinct_prefix(key, DEVS, N_NODE * CAPN)
    return chosen.reshape(DEVS, N_NODE, CAPN).astype(jnp.int32)


def draw_domain_sends(key, part):
    key = jax.random.fold_in(key, 47)
    chosen = distinct_prefix(key, DEVS * 2, CAPD)
    return chosen.reshape(DEVS, 2, CAPD).astype(jnp.int32)


def plant(result, own_key, least, high):
    spot = [jax.random.randint(jax.random.fold_in(own_key, axis), (), 0, length) for axis, length in enumerate(result.shape)]
    longest = result.shape.index(max(result.shape))
    neighbour = spot[:longest] + [(spot[longest] + 1) % result.shape[longest]] + spot[longest + 1:]
    return result.at[tuple(spot)].set(least).at[tuple(neighbour)].set(high)


def level_of(rng, extent, cuts, low, top_value):
    factor_of = 1.0
    for position, blocks in cuts:
        heights = jax.random.uniform(jax.random.fold_in(jax.random.fold_in(rng, 6), position), (blocks,), jnp.float32, low / len(cuts), top_value / len(cuts))
        factor_of = factor_of * jnp.repeat(jnp.exp(heights), extent[position] // blocks).reshape((-1,) + (1,) * (len(extent) - 1 - position))
    return factor_of


def gaussian(key, shape, scale, bound, shards=(), kind=jnp.bfloat16):
    loudness = level_of(key, shape, shards, -0.22, 0.18) if shards else 1.0
    drawn = jax.random.normal(key, shape, jnp.float32) * scale * loudness
    return jnp.minimum(jnp.maximum(drawn, -bound), bound).astype(kind)


def setup_inputs(seed: int = 0) -> dict:
    splits = jax.random.split(jax.random.key(seed), 9)
    positions = gaussian(splits[0], (3, PARTICLES), 1.0, 6.0, ((1, 32),), jnp.float32)
    masses = jnp.clip(jnp.exp(math.log(2.0) - 1.3862944 * jax.random.uniform(splits[1], (PARTICLES,), jnp.float32) ** level_of(splits[1], (PARTICLES,), ((0, 32),), -0.2, 0.2)), 0.5, 2.0)
    metric = draw_metric(jax.random.fold_in(splits[8], 71), 0)
    energy = jnp.clip(jnp.exp(math.log(2.0) - 1.3862944 * jax.random.uniform(splits[3], (PARTICLES,), jnp.float32) ** level_of(splits[3], (PARTICLES,), ((0, 32),), -0.2, 0.2)), 0.5, 2.0)
    local_pairs = plant(jax.random.randint(splits[4], (BLOCKS, KL), 0, NB), jax.random.fold_in(splits[4], 1), 0, NB - 1).astype(jnp.int32)
    ghost_pairs = jax.vmap(lambda own: jax.random.permutation(own, GHOSTS))(jax.random.split(splits[5], DEVS)).reshape((DEVS, GHOSTS)).astype(jnp.int32)
    node_sends = draw_node_sends(jax.random.fold_in(splits[8], 71), 0)
    domain_sends = draw_domain_sends(jax.random.fold_in(splits[8], 71), 0)
    return {"positions": positions, "masses": masses, "metric": metric, "energy": energy, "local_pairs": local_pairs, "ghost_pairs": ghost_pairs, "node_sends": node_sends, "domain_sends": domain_sends}


ADIABATIC = 5.0 / 3.0
TARGET_SCALE = 0.5
RIDGE_TERM = 0.1

def quad_form(metric, offset):
    return metric[0] * offset[0] * offset[0] + metric[1] * offset[1] * offset[1] + metric[2] * offset[2] * offset[2] + 2.0 * (metric[3] * offset[0] * offset[1] + metric[4] * offset[0] * offset[2] + metric[5] * offset[1] * offset[2])

def apply_metric(metric, offset):
    return jnp.stack([metric[0] * offset[0] + metric[3] * offset[1] + metric[4] * offset[2], metric[3] * offset[0] + metric[1] * offset[1] + metric[5] * offset[2], metric[4] * offset[0] + metric[5] * offset[1] + metric[2] * offset[2]])

def contract_own(weights, features):
    return jnp.einsum('bij,kbj->kbi', weights, features, precision=lax.Precision.HIGHEST)

def contract_back(weights, features):
    return jnp.einsum('bij,kbi->kbj', weights, features, precision=lax.Precision.HIGHEST)

def moment_features(fields):
    place = fields[0:3]
    mass = fields[3]
    return mass[None] * jnp.stack([jnp.ones_like(mass), place[0], place[1], place[2], place[0] * place[0], place[1] * place[1], place[2] * place[2], place[0] * place[1], place[0] * place[2], place[1] * place[2]])

def spread_moments(sums, place):
    total = sums[0]

    def second(first_pos, other_pos, first_sum, other_sum, joint_sum):
        return first_pos * other_pos * total - first_pos * other_sum - other_pos * first_sum + joint_sum
    return jnp.stack([total, second(place[0], place[0], sums[1], sums[1], sums[4]), second(place[1], place[1], sums[2], sums[2], sums[5]), second(place[2], place[2], sums[3], sums[3], sums[6]), second(place[0], place[1], sums[1], sums[2], sums[7]), second(place[0], place[2], sums[1], sums[3], sums[8]), second(place[1], place[2], sums[2], sums[3], sums[9])])

def mass_features(fields):
    mass = fields[3]
    return jnp.stack([mass, mass * fields[0], mass * fields[1], mass * fields[2]])

def force_features(fields):
    scale = 4.0 * fields[3] * fields[10]
    metric = fields[4:10]
    return scale[None] * jnp.concatenate([metric, apply_metric(metric, fields[0:3])], axis=0)

def pair_terms(pass_kind, own_fields, partner_fields):
    offset = own_fields[0:3, :, :, None] - partner_fields[0:3, :, None, :]
    quad_own = 1.0 + quad_form(own_fields[4:10, :, :, None], offset)
    quad_partner = 1.0 + quad_form(partner_fields[4:10, :, None, :], offset)
    own_place = own_fields[0:3]
    partner_place = partner_fields[0:3]
    if pass_kind == 'moments':
        weight_own = 1.0 / jnp.square(quad_own)
        weight_partner = 1.0 / jnp.square(quad_partner)
        own_side = spread_moments(contract_own(weight_own, moment_features(partner_fields)), own_place)
        partner_side = spread_moments(contract_back(weight_partner, moment_features(own_fields)), partner_place)
    elif pass_kind == 'density':
        own_side = contract_own(1.0 / jnp.square(quad_own), partner_fields[3:4])
        partner_side = contract_back(1.0 / jnp.square(quad_partner), own_fields[3:4])
    else:
        cube_own = 1.0 / (quad_own * quad_own * quad_own)
        cube_partner = 1.0 / (quad_partner * quad_partner * quad_partner)
        first = contract_own(cube_own, mass_features(partner_fields))
        term_own = (4.0 * own_fields[10])[None] * apply_metric(own_fields[4:10], own_place * first[0:1] - first[1:4])
        second = contract_own(cube_partner, force_features(partner_fields))
        term_cross = apply_metric(second[0:6], own_place) - second[6:9]
        third = contract_back(cube_own, force_features(own_fields))
        term_back = apply_metric(third[0:6], partner_place) - third[6:9]
        fourth = contract_back(cube_partner, mass_features(own_fields))
        term_partner = (4.0 * partner_fields[10])[None] * apply_metric(partner_fields[4:10], partner_place * fourth[0:1] - fourth[1:4])
        own_side = term_own + term_cross
        partner_side = term_back + term_partner
    return (own_side, partner_side)

def inverse_parts(matrix):
    cofactors = jnp.stack([matrix[1] * matrix[2] - matrix[5] * matrix[5], matrix[0] * matrix[2] - matrix[4] * matrix[4], matrix[0] * matrix[1] - matrix[3] * matrix[3], matrix[4] * matrix[5] - matrix[3] * matrix[2], matrix[3] * matrix[5] - matrix[4] * matrix[1], matrix[3] * matrix[4] - matrix[0] * matrix[5]])
    determinant = matrix[0] * cofactors[0] + matrix[3] * cofactors[3] + matrix[4] * cofactors[4]
    return (cofactors, determinant)

def next_metric(metric, moment_sums):
    spread = moment_sums[1:] / moment_sums[0]
    ridge_diag = jnp.array([RIDGE_TERM, RIDGE_TERM, RIDGE_TERM, 0.0, 0.0, 0.0], jnp.float32)[:, None, None]
    cofactors, determinant = inverse_parts(spread + ridge_diag)
    return 0.5 * metric + 0.5 * TARGET_SCALE * cofactors / determinant

def global_pass(pass_kind, fields, partner, field_count):
    blocks = fields.shape[1] - 1
    group_size = 4 * NB
    own_fields = fields[:, :blocks]
    running = jnp.zeros((field_count, blocks + 1, P_SIZE), jnp.float32)

    def one_group(operands):
        return pair_terms(pass_kind, operands[0], operands[1])

    def to_groups(stacked):
        return jnp.moveaxis(stacked.reshape(stacked.shape[0], blocks // group_size, group_size, P_SIZE), 1, 0)

    def from_groups(stacked):
        return jnp.moveaxis(stacked, 0, 1).reshape(field_count, blocks, P_SIZE)
    for column in range(KL + KG):
        partner_rows = partner[:, column]
        partner_fields = fields[:, partner_rows]
        own_side, partner_side = lax.map(one_group, (to_groups(own_fields), to_groups(partner_fields)))
        running = running.at[:, :blocks].add(from_groups(own_side))
        running = running.at[:, partner_rows].add(from_groups(partner_side))
    return running[:, :blocks]

def ghost_blocks(node_sends, domain_sends):
    device = jnp.arange(DEVS, dtype=jnp.int32)
    domain = device // N_NODE
    node_index = device % N_NODE
    sources = domain[:, None] * N_NODE + jnp.arange(N_NODE, dtype=jnp.int32)[None, :]
    node_blocks = node_sends[sources, node_index[:, None], :] + sources[:, :, None] * NB
    lower_valid = domain > 0
    upper_valid = domain < N_DOM - 1
    lower_source = jnp.where(lower_valid, device - N_NODE, 0).astype(jnp.int32)
    upper_source = jnp.where(upper_valid, device + N_NODE, 0).astype(jnp.int32)
    lower_blocks = jnp.where(lower_valid[:, None], domain_sends[lower_source, 1, :] + lower_source[:, None] * NB, BLOCKS)
    upper_blocks = jnp.where(upper_valid[:, None], domain_sends[upper_source, 0, :] + upper_source[:, None] * NB, BLOCKS)
    return jnp.concatenate([node_blocks.reshape(DEVS, N_NODE * CAPN), lower_blocks, upper_blocks], axis=1).astype(jnp.int32)

def metric_det(matrix):
    cofactors, determinant = inverse_parts(matrix)
    return determinant

def reference(positions, masses, metric, energy, local_pairs, ghost_pairs, node_sends, domain_sends):
    ghosts = ghost_blocks(node_sends, domain_sends)
    block_base = jnp.arange(BLOCKS, dtype=jnp.int32) // NB * NB
    local_global = (local_pairs + block_base[:, None]).astype(jnp.int32)
    ghost_global = jnp.take_along_axis(ghosts, ghost_pairs, axis=1).reshape(BLOCKS, KG).astype(jnp.int32)
    partner = jnp.concatenate([local_global, ghost_global], axis=1)
    pos_blocks = positions.reshape(3, BLOCKS, P_SIZE)
    mass_blocks = masses.reshape(1, BLOCKS, P_SIZE)
    current_metric = metric.reshape(6, BLOCKS, P_SIZE)
    padding = jnp.zeros((11, 1, P_SIZE), jnp.float32)
    for iteration in range(ITERS):
        fields = jnp.concatenate([pos_blocks, mass_blocks, current_metric], axis=0)
        fields = jnp.concatenate([fields, padding[:10]], axis=1)
        moment_sums = global_pass('moments', fields, partner, 7)
        current_metric = next_metric(current_metric, moment_sums)
    fields = jnp.concatenate([pos_blocks, mass_blocks, current_metric], axis=0)
    fields = jnp.concatenate([fields, padding[:10]], axis=1)
    density_sum = global_pass('density', fields, partner, 1)[0]
    volume = jnp.sqrt(metric_det(current_metric)) / (P_SIZE * (KL + KG))
    density = volume * density_sum
    coefficient = (ADIABATIC - 1.0) * energy.reshape(BLOCKS, P_SIZE) / density * volume
    fields = jnp.concatenate([pos_blocks, mass_blocks, current_metric, coefficient[None]], axis=0)
    fields = jnp.concatenate([fields, padding], axis=1)
    acceleration = global_pass('force', fields, partner, 3)
    return (current_metric.reshape(6, PARTICLES), density.reshape(PARTICLES), acceleration.reshape(3, PARTICLES))
```

```python
import functools

import jax
import jax.numpy as jnp
from jax import lax
from jax.experimental import pallas as pl
from jax.experimental.pallas import tpu as pltpu
from jax.sharding import PartitionSpec as P

SIZE = 128
KG = 2
LISTED = 3
ITERS = 3
STEPS = 8
AHEAD = 2
ADIABATIC = 5.0 / 3.0
TARGET_SCALE = 0.5
RIDGE_TERM = 0.1
TERMS = 10
HALF = 64
MESH = pl.DeviceIdType.MESH
F32 = jnp.float32
BF16 = jnp.bfloat16


def lanes(block, count=1):
    return pl.ds(pl.multiple_of(block * SIZE, SIZE), count * SIZE)


def greet(n_dom, n_node):
    a, c = lax.axis_index("dom"), lax.axis_index("node")
    barrier = pltpu.get_barrier_semaphore()
    for turn in range(1, n_node):
        pl.semaphore_signal(
            barrier, inc=1, device_id=(a, lax.rem(c + turn, n_node)), device_id_type=MESH
        )

    @pl.when(a > 0)
    def _():
        pl.semaphore_signal(barrier, inc=1, device_id=(a - 1, c), device_id_type=MESH)

    @pl.when(a < n_dom - 1)
    def _():
        pl.semaphore_signal(barrier, inc=1, device_id=(a + 1, c), device_id_type=MESH)

    inner = (a > 0).astype(jnp.int32) + (a < n_dom - 1).astype(jnp.int32)
    pl.semaphore_wait(barrier, n_node - 1 + inner)


def static_exchange(
    n_dom, n_node, pos_ref, mass_ref, node_ref, domain_ref, ghost_ref, recv_ref, rtab_ref, send, land
):
    a, c = lax.axis_index("dom"), lax.axis_index("node")
    prev_slot, next_slot = n_node, n_node + 1
    recv_ref[c, 0:3, :] = pos_ref[...]
    recv_ref[c, 3:4, :] = mass_ref[...]
    rtab_ref[c] = jnp.zeros(rtab_ref.shape[1:], jnp.int32)
    capn = node_ref.shape[1]
    rtab_ref[c, 0:capn, 0:n_node] = node_ref[0]
    rtab_ref[c, capn:capn + 2, 0:domain_ref.shape[2]] = domain_ref[0]
    rtab_ref[c, capn + 2:capn + 3, 0:ghost_ref.shape[1]] = ghost_ref[...]

    @pl.when(a == 0)
    def _():
        recv_ref[prev_slot] = jnp.zeros(recv_ref.shape[1:], F32)
        rtab_ref[prev_slot] = jnp.zeros(rtab_ref.shape[1:], jnp.int32)

    @pl.when(a == n_dom - 1)
    def _():
        recv_ref[next_slot] = jnp.zeros(recv_ref.shape[1:], F32)
        rtab_ref[next_slot] = jnp.zeros(rtab_ref.shape[1:], jnp.int32)

    greet(n_dom, n_node)

    def copies(lane, target, slot):
        return [
            pltpu.make_async_remote_copy(
                src_ref=ref.at[c],
                dst_ref=ref.at[slot],
                send_sem=send.at[lane, part],
                recv_sem=land.at[lane, part],
                device_id=target,
                device_id_type=MESH,
            )
            for part, ref in enumerate((recv_ref, rtab_ref))
        ]

    to_prev = copies(0, (a - 1, c), next_slot)
    to_next = copies(1, (a + 1, c), prev_slot)
    around = [
        copies(1 + turn, (a, lax.rem(c + turn, n_node)), c) for turn in range(1, n_node)
    ]
    finish(a, n_dom, to_prev, to_next, around)


def finish(a, n_dom, to_prev, to_next, around):
    @pl.when(a > 0)
    def _():
        for copy in to_prev:
            copy.start()

    @pl.when(a < n_dom - 1)
    def _():
        for copy in to_next:
            copy.start()

    for group in around:
        for copy in group:
            copy.start()
    for group in around:
        for copy in group:
            copy.wait()

    @pl.when(a > 0)
    def _():
        for copy in to_prev:
            copy.wait_send()
        for copy in to_next:
            copy.wait_recv()

    @pl.when(a < n_dom - 1)
    def _():
        for copy in to_next:
            copy.wait_send()
        for copy in to_prev:
            copy.wait_recv()


def term_exchange(n_dom, n_node, capn, capd, pay_ref, recv_ref, send, land):
    a, c = lax.axis_index("dom"), lax.axis_index("node")
    first = n_node * capn
    prev_cols = pl.ds(first * SIZE, capd * SIZE)
    next_cols = pl.ds((first + capd) * SIZE, capd * SIZE)
    recv_ref[:, lanes(c * capn, capn)] = pay_ref[:, lanes(c * capn, capn)]

    @pl.when(a == 0)
    def _():
        recv_ref[:, prev_cols] = jnp.zeros((8, capd * SIZE), F32)

    @pl.when(a == n_dom - 1)
    def _():
        recv_ref[:, next_cols] = jnp.zeros((8, capd * SIZE), F32)

    greet(n_dom, n_node)

    def copies(lane, target, src, dst):
        return [
            pltpu.make_async_remote_copy(
                src_ref=pay_ref.at[:, src],
                dst_ref=recv_ref.at[:, dst],
                send_sem=send.at[lane],
                recv_sem=land.at[lane],
                device_id=target,
                device_id_type=MESH,
            )
        ]

    to_prev = copies(0, (a - 1, c), prev_cols, next_cols)
    to_next = copies(1, (a + 1, c), next_cols, prev_cols)
    around = []
    for turn in range(1, n_node):
        peer = lax.rem(c + turn, n_node)
        around.append(copies(1 + turn, (a, peer), lanes(peer * capn, capn), lanes(c * capn, capn)))
    finish(a, n_dom, to_prev, to_next, around)


def set_parts(out, base, values, order):
    count = values[0].shape[0]
    for k, value in enumerate(values):
        high = value.astype(BF16).astype(F32)
        rest = value - high
        middle = rest.astype(BF16).astype(F32)
        parts = (high, middle, rest - middle)
        for group, part in enumerate(order):
            at = base + (TERMS * group + k) * count
            out[at:at + count, :] = parts[part]


def split2(value):
    high = value.astype(BF16)
    return high, (value - high.astype(F32)).astype(BF16)


def dot(left, right):
    return jnp.dot(left, right, preferred_element_type=F32)


def inverse_parts(m):
    cofactors = [
        m[1] * m[2] - m[5] * m[5],
        m[0] * m[2] - m[4] * m[4],
        m[0] * m[1] - m[3] * m[3],
        m[4] * m[5] - m[3] * m[2],
        m[3] * m[5] - m[4] * m[1],
        m[3] * m[4] - m[0] * m[5],
    ]
    return cofactors, m[0] * cofactors[0] + m[3] * cofactors[3] + m[4] * cofactors[4]


def apply_metric(m, x):
    return [
        m[0] * x[0] + m[3] * x[1] + m[4] * x[2],
        m[3] * x[0] + m[1] * x[1] + m[5] * x[2],
        m[4] * x[0] + m[5] * x[1] + m[2] * x[2],
    ]


def inverse_of(s):
    return pltpu.reciprocal(s, approx=True)


def compute(
    sizes,
    tab_ref, local_ref, recv_ref, metric_ref, energy_ref,
    final_ref, density_ref, accel_ref, pay_ref,
    held, src, pack, low_t, high_t, twin_t, feat_m, narrow, coef, acc, thirds_acc, cubes, back_feat, backs, own,
):
    n_node, capn, capd, blocks = sizes
    ghosts = blocks * KG
    sources = blocks + 2 * ghosts
    first = n_node * capn
    ghost_row = capn + 2
    slots = n_node + 2
    c = lax.axis_index("node")

    def strided(n, count, stride):
        return pl.ds(n, count, stride=stride)

    for slot in range(slots):
        if slot >= n_node:
            @pl.loop(0, ghosts, unroll=8)
            def _(n, slot=slot):
                held[slot, n] = 0

        @pl.loop(0, ghosts, unroll=8)
        def _(n, slot=slot):
            held[slot, tab_ref[slot, ghost_row, n]] = n // KG

    for n in range(blocks):
        at = slice(n * SIZE, (n + 1) * SIZE)
        src[strided(n, 4, sources), :] = recv_ref[c, :, at]
        own[strided(n, 6, blocks), :] = metric_ref[:, at]
        own[6 * blocks + n:6 * blocks + n + 1, :] = energy_ref[:, at]

    for n in range(ghosts):
        slot = tab_ref[c, ghost_row, n]
        near = slot < first
        low = slot < first + capd
        past = slot - first
        from_slot = jnp.where(near, slot // capn, jnp.where(low, n_node, n_node + 1))
        row = jnp.where(near, slot % capn, jnp.where(low, capn + 1, capn))
        col = jnp.where(near, c, jnp.where(low, past, past - capd))
        block = tab_ref[from_slot, row, col]
        src[strided(blocks + n, 4, sources), :] = recv_ref[from_slot, :, lanes(block)]

    for n in range(ghosts):
        if n < first:
            from_slot, there = n // capn, c * capn + n % capn
        elif n < first + capd:
            from_slot, there = n_node, n + capd
        else:
            from_slot, there = n_node + 1, n - capd
        block = held[from_slot, there]
        src[strided(blocks + ghosts + n, 4, sources), :] = recv_ref[from_slot, :, lanes(block)]

    def send_target(n):
        near = n < first
        low = n < first + capd
        past = n - first
        row = jnp.where(near, n % capn, jnp.where(low, capn, capn + 1))
        return tab_ref[c, row, jnp.where(near, n // capn, jnp.where(low, past, past - capd))]

    x, y, z, mass = (src[k * sources:(k + 1) * sources, :] for k in range(4))
    feature = [jnp.ones_like(x), x, y, z, x * x, y * y, z * z, x * y, x * z, y * z]
    pack[60 * sources:, :] = jnp.zeros((4 * sources, SIZE), F32)
    set_parts(pack, 0, feature, (0, 1, 0, 2, 1, 0))
    blank = jnp.zeros((HALF, SIZE), BF16)

    @pl.loop(0, blocks, unroll=4)
    def _(n):
        one = pack[strided(n, HALF, sources), :].astype(BF16)
        low_t[n] = jnp.concatenate([one, blank], axis=0).T
        high_t[n] = jnp.concatenate([blank, one], axis=0).T

    @pl.loop(0, ghosts, unroll=4)
    def _(n):
        one = pack[strided(blocks + 2 * n, HALF, sources), :].astype(BF16)
        other = pack[strided(blocks + 2 * n + 1, HALF, sources), :].astype(BF16)
        twin_t[n] = jnp.concatenate([one, other], axis=0).T

    pack[30 * sources:32 * sources, :] = jnp.zeros((2 * sources, SIZE), F32)
    set_parts(pack, 0, [row * mass for row in feature], (0, 1, 2))

    @pl.loop(0, sources, unroll=8)
    def _(n):
        feat_m[n] = pack[strided(n, 32, sources), :].astype(BF16)

    def set_coefficients(g, r):
        gr = apply_metric(g, r)
        rows = [
            1.0 + gr[0] * r[0] + gr[1] * r[1] + gr[2] * r[2],
            -2.0 * gr[0], -2.0 * gr[1], -2.0 * gr[2],
            g[0], g[1], g[2], 2.0 * g[3], 2.0 * g[4], 2.0 * g[5],
        ]
        set_parts(narrow, 0, rows, (0, 0, 1, 0, 1, 2))
        for t in range(blocks):
            coef[t] = narrow[strided(t, HALF, blocks), :].astype(BF16)

    def units(e):
        local = local_ref[0, e]
        sent = [send_target(KG * e + k) for k in range(KG)]
        ghost, back = blocks + KG * e, blocks + ghosts + KG * e
        return [
            ((e, ghost), (e, ghost + 1)),
            ((sent[0], back), (sent[1], back + 1)),
            ((e, local), (local, e)),
        ]

    def quads(e, kind, unit):
        if kind == 0:
            left = twin_t[e]
        elif kind == 1:
            left = twin_t[blocks + e]
        else:
            left = low_t[unit[0][1]] + high_t[unit[1][1]]
        none = jnp.zeros((HALF, SIZE), BF16)
        top = jnp.concatenate([coef[unit[0][0]], none], axis=1)
        bottom = jnp.concatenate([none, coef[unit[1][0]]], axis=1)
        return dot(left, jnp.concatenate([top, bottom], axis=0))

    def mass_rows(unit):
        one, other = (feat_m[source] for _, source in unit)
        return jnp.concatenate(
            [jnp.concatenate([one, one], axis=1), jnp.concatenate([other, other], axis=1)], axis=0
        )

    def stacked(value):
        return jnp.concatenate(split2(value), axis=0)

    def listed_units(e):
        return [
            (e + step, kind, unit)
            for step in range(STEPS)
            for kind, unit in enumerate(units(e + step))
        ]

    def ahead(listed):
        waiting = []
        for index, item in enumerate(listed):
            waiting.append(quads(*item))
            if index >= AHEAD:
                yield index - AHEAD, listed[index - AHEAD], inverse_of(waiting[index - AHEAD])
        for index in range(max(len(listed) - AHEAD, 0), len(listed)):
            yield index, listed[index], inverse_of(waiting[index])

    def rows_of(block):
        return pl.ds(pl.multiple_of(block * 32, 32), 32)

    def add_sums(into, listed, sums):
        for (e, kind, unit), value in zip(listed, sums):
            one, other = value[0:32, 0:SIZE], value[32:64, SIZE:2 * SIZE]
            if kind == 0:
                into[rows_of(e), :] += one + other
            else:
                into[rows_of(unit[0][0]), :] += one
                into[rows_of(unit[1][0]), :] += other

    def summed(ref, k, count):
        low, middle, high = (ref[strided(k + TERMS * part, count, 32), :] for part in (2, 1, 0))
        return high + (middle + low)

    def place():
        return [src[k * sources:k * sources + blocks, :] for k in range(3)]

    def metric():
        return [own[k * blocks:(k + 1) * blocks, :] for k in range(6)]

    narrow[60 * blocks:, :] = jnp.zeros((4 * blocks, SIZE), F32)

    @pl.loop(0, ITERS)
    def _(iteration):
        g, r = metric(), place()
        set_coefficients(g, r)
        acc[...] = jnp.zeros(acc.shape, F32)

        @pl.loop(0, blocks, step=STEPS)
        def _(e):
            listed = listed_units(e)
            sums = []
            for _, (_, _, unit), inv in ahead(listed):
                sums.append(dot(mass_rows(unit), stacked(inv * inv)))
            add_sums(acc, listed, sums)

        s = [summed(acc, k, blocks) for k in range(TERMS)]
        g, r = metric(), place()
        total = s[0]
        share = 1.0 / total

        def second(i, j, at):
            return (r[i] * r[j] * total - r[i] * s[1 + j] - r[j] * s[1 + i] + s[at]) * share

        spread = [
            second(0, 0, 4) + RIDGE_TERM,
            second(1, 1, 5) + RIDGE_TERM,
            second(2, 2, 6) + RIDGE_TERM,
            second(0, 1, 7),
            second(0, 2, 8),
            second(1, 2, 9),
        ]
        cofactors, determinant = inverse_parts(spread)
        weight = 0.5 * TARGET_SCALE / determinant
        for k in range(6):
            own[k * blocks:(k + 1) * blocks, :] = 0.5 * g[k] + cofactors[k] * weight

    set_coefficients(metric(), place())
    acc[...] = jnp.zeros(acc.shape, F32)
    thirds_acc[...] = jnp.zeros(thirds_acc.shape, F32)

    @pl.loop(0, blocks, step=STEPS)
    def _(e):
        listed = listed_units(e)
        squares, thirds = [], []
        for index, (_, _, unit), inv in ahead(listed):
            square = inv * inv
            cube = stacked(square * inv)
            cubes[3 * e + index] = cube
            left = mass_rows(unit)
            squares.append(dot(left, stacked(square)))
            thirds.append(dot(left, cube))
        add_sums(acc, listed, squares)
        add_sums(thirds_acc, listed, thirds)

    g, r = metric(), place()
    cofactors, determinant = inverse_parts(g)
    volume = jnp.sqrt(determinant) / (SIZE * LISTED)
    density = volume * summed(acc, 0, blocks)
    energy = own[6 * blocks:7 * blocks, :]
    coefficient = (ADIABATIC - 1.0) * energy / density * volume
    scale = 4.0 * src[3 * sources:3 * sources + blocks, :] * coefficient
    own[6 * blocks:7 * blocks, :] = density
    own[7 * blocks:8 * blocks, :] = coefficient
    set_parts(narrow, 0, [scale * row for row in g + apply_metric(g, r) + [jnp.zeros_like(scale)]], (0, 1, 2))
    narrow[30 * blocks:32 * blocks, :] = jnp.zeros((2 * blocks, SIZE), F32)
    for t in range(blocks):
        back_feat[t] = narrow[strided(t, 32, blocks), :].astype(BF16)
    backs[0:32 * blocks, :] = jnp.zeros((32 * blocks, SIZE), F32)

    @pl.loop(0, blocks, step=STEPS)
    def _(e):
        listed = listed_units(e)
        values = []
        for index, (at, kind, unit) in enumerate(listed):
            one, other = (back_feat[target] for target, _ in unit)
            none = jnp.zeros((32, SIZE), BF16)
            left = jnp.concatenate(
                [jnp.concatenate([one, none], axis=1), jnp.concatenate([none, other], axis=1)], axis=0
            )
            value = lax.dot_general(
                left, cubes[3 * e + index], (((1,), (1,)), ((), ())), preferred_element_type=F32
            )
            values.append(value[:, 0:SIZE] + value[:, SIZE:2 * SIZE])
        for (_, kind, unit), value in zip(listed, values):
            for half, (_, source) in enumerate(unit):
                if kind < 2:
                    backs[rows_of(source), :] = value[32 * half:32 * half + 32]
        for (_, kind, unit), value in zip(listed, values):
            for half, (_, source) in enumerate(unit):
                if kind == 2:
                    backs[rows_of(source), :] += value[32 * half:32 * half + 32]

    b = [summed(backs, k, sources) for k in range(9)]
    where = [src[k * sources:(k + 1) * sources, :] for k in range(3)]
    back = [moved - b[6 + k] for k, moved in enumerate(apply_metric(b[0:6], where))]
    f = [summed(thirds_acc, k, blocks) for k in range(4)]
    g, r = metric(), place()
    coefficient = own[7 * blocks:8 * blocks, :]
    forward = apply_metric(g, [r[k] * f[0] - f[1 + k] for k in range(3)])
    for k in range(3):
        pack[k * sources:(k + 1) * sources, :] = back[k]
        narrow[k * blocks:(k + 1) * blocks, :] = 4.0 * coefficient * forward[k] + back[k][0:blocks]
    for t in range(blocks):
        at = slice(t * SIZE, (t + 1) * SIZE)
        final_ref[:, at] = own[strided(t, 6, blocks), :]
        density_ref[:, at] = own[6 * blocks + t:6 * blocks + t + 1, :]
        accel_ref[:, at] = narrow[strided(t, 3, blocks), :]

    for n in range(ghosts):
        pay_ref[4:7, n * SIZE:(n + 1) * SIZE] = pack[strided(blocks + ghosts + n, 3, sources), :]
        slot = tab_ref[c, ghost_row, n]
        pay_ref[0:3, lanes(slot)] = pack[strided(blocks + n, 3, sources), :]


def add_terms(sizes, tab_ref, part_ref, recv_ref, out_ref):
    n_node, capn, capd, blocks = sizes
    c = lax.axis_index("node")
    out_ref[...] = part_ref[...]
    for n in range(blocks * KG):
        past = n - n_node * capn
        row, col = (n % capn, n // capn) if past < 0 else (capn + past // capd, past % capd)
        at = slice(n * SIZE, (n + 1) * SIZE)
        out_ref[:, lanes(tab_ref[c, row, col])] += recv_ref[0:3, at]
    for e in range(blocks):
        at = slice(e * SIZE, (e + 1) * SIZE)
        terms = [recv_ref[4:7, lanes(tab_ref[c, capn + 2, KG * e + k])] for k in range(KG)]
        out_ref[:, at] += sum(terms[1:], terms[0])


def on_device(n_dom, n_node, positions, masses, metric, energy, local_pairs, ghost_pairs, node_sends, domain_sends):
    blocks = local_pairs.shape[0]
    capn, capd = node_sends.shape[2], domain_sends.shape[2]
    ghosts = blocks * KG
    width = blocks * SIZE
    sources = blocks + 2 * ghosts
    slots = n_node + 2
    sizes = (n_node, capn, capd, blocks)
    rows = -(-(capn + 3) // 8) * 8
    vmem = pl.BlockSpec(memory_space=pltpu.VMEM)
    smem = pl.BlockSpec(memory_space=pltpu.SMEM)
    received, tables = pl.pallas_call(
        functools.partial(static_exchange, n_dom, n_node),
        out_shape=(
            jax.ShapeDtypeStruct((slots, 4, width), F32),
            jax.ShapeDtypeStruct((slots, rows, SIZE), jnp.int32),
        ),
        in_specs=[vmem] * 5,
        out_specs=(vmem, vmem),
        scratch_shapes=[
            pltpu.SemaphoreType.DMA((n_node + 1, 2)),
            pltpu.SemaphoreType.DMA((n_node + 1, 2)),
        ],
        compiler_params=pltpu.CompilerParams(collective_id=0, has_side_effects=True),
        name="static_exchange",
    )(positions, masses.reshape(1, width), node_sends.swapaxes(1, 2), domain_sends, ghost_pairs)
    final, density, part, pay = pl.pallas_call(
        functools.partial(compute, sizes),
        out_shape=(
            jax.ShapeDtypeStruct((6, width), F32),
            jax.ShapeDtypeStruct((1, width), F32),
            jax.ShapeDtypeStruct((3, width), F32),
            jax.ShapeDtypeStruct((8, ghosts * SIZE), F32),
        ),
        in_specs=[smem, smem, vmem, vmem, vmem],
        out_specs=(vmem,) * 4,
        scratch_shapes=[
            pltpu.SMEM((slots, ghosts), jnp.int32),
            pltpu.VMEM((4 * sources, SIZE), F32),
            pltpu.VMEM((HALF * sources, SIZE), F32),
            pltpu.VMEM((blocks, SIZE, SIZE), BF16),
            pltpu.VMEM((blocks, SIZE, SIZE), BF16),
            pltpu.VMEM((ghosts, SIZE, SIZE), BF16),
            pltpu.VMEM((sources, 32, SIZE), BF16),
            pltpu.VMEM((HALF * blocks, SIZE), F32),
            pltpu.VMEM((blocks, HALF, SIZE), BF16),
            pltpu.VMEM((32 * blocks, SIZE), F32),
            pltpu.VMEM((32 * blocks, SIZE), F32),
            pltpu.VMEM((3 * blocks, 2 * SIZE, 2 * SIZE), BF16),
            pltpu.VMEM((blocks, 32, SIZE), BF16),
            pltpu.VMEM((32 * sources, SIZE), F32),
            pltpu.VMEM((8 * blocks, SIZE), F32),
        ],
        compiler_params=pltpu.CompilerParams(vmem_limit_bytes=62 * 2**20),
        name="compute",
    )(tables, local_pairs.T, received, metric, energy.reshape(1, width))
    returned = pl.pallas_call(
        functools.partial(term_exchange, n_dom, n_node, capn, capd),
        out_shape=jax.ShapeDtypeStruct((8, ghosts * SIZE), F32),
        in_specs=[vmem],
        out_specs=vmem,
        scratch_shapes=[
            pltpu.SemaphoreType.DMA((n_node + 1,)),
            pltpu.SemaphoreType.DMA((n_node + 1,)),
        ],
        compiler_params=pltpu.CompilerParams(collective_id=1, has_side_effects=True),
        name="term_exchange",
    )(pay)
    accel = pl.pallas_call(
        functools.partial(add_terms, sizes),
        out_shape=jax.ShapeDtypeStruct((3, width), F32),
        in_specs=[smem, vmem, vmem],
        out_specs=vmem,
        name="add_terms",
    )(tables, part, returned)
    return (final, density.reshape(-1), accel)


def solution(mesh):
    in_specs = (
        P(None, ("dom", "node")),
        P(("dom", "node")),
        P(None, ("dom", "node")),
        P(("dom", "node")),
        P(("dom", "node"), None),
        P(("dom", "node"), None),
        P(("dom", "node"), None, None),
        P(("dom", "node"), None, None),
    )
    out_specs = (P(None, ("dom", "node")), P(("dom", "node")), P(None, ("dom", "node")))
    return jax.shard_map(
        functools.partial(on_device, mesh.shape["dom"], mesh.shape["node"]),
        mesh=mesh, in_specs=in_specs, out_specs=out_specs, check_vma=False,
    )
```

```python
import functools

import jax
import jax.numpy as jnp
from jax import lax
from jax.experimental import pallas as pl
from jax.experimental.pallas import tpu as pltpu
from jax.sharding import PartitionSpec as P

SIZE = 128
KG = 2
LISTED = 3
ITERS = 3
STEPS = 16
AHEAD = 4
ADIABATIC = 5.0 / 3.0
TARGET_SCALE = 0.5
RIDGE_TERM = 0.1
TERMS = 10
HALF = 64
MESH = pl.DeviceIdType.MESH
F32 = jnp.float32
BF16 = jnp.bfloat16


def lanes(block, count=1):
    return pl.ds(pl.multiple_of(block * SIZE, SIZE), count * SIZE)


def greet(n_dom, n_node):
    a, c = lax.axis_index("dom"), lax.axis_index("node")
    barrier = pltpu.get_barrier_semaphore()
    for turn in range(1, n_node):
        pl.semaphore_signal(
            barrier, inc=1, device_id=(a, lax.rem(c + turn, n_node)), device_id_type=MESH
        )

    @pl.when(a > 0)
    def _():
        pl.semaphore_signal(barrier, inc=1, device_id=(a - 1, c), device_id_type=MESH)

    @pl.when(a < n_dom - 1)
    def _():
        pl.semaphore_signal(barrier, inc=1, device_id=(a + 1, c), device_id_type=MESH)

    inner = (a > 0).astype(jnp.int32) + (a < n_dom - 1).astype(jnp.int32)
    pl.semaphore_wait(barrier, n_node - 1 + inner)


def static_exchange(
    n_dom, n_node, pos_ref, mass_ref, node_ref, domain_ref, ghost_ref, recv_ref, rmass_ref, rtab_ref,
    tab, none, no_tab, send, land, local,
):
    a, c = lax.axis_index("dom"), lax.axis_index("node")
    prev_slot, next_slot = n_node, n_node + 1
    capn = node_ref.shape[1]
    none[...] = jnp.zeros(none.shape, F32)
    no_tab[...] = jnp.zeros(no_tab.shape, jnp.int32)
    tab[...] = jnp.zeros(tab.shape, jnp.int32)
    tab[0:capn, 0:n_node] = node_ref[0]
    tab[capn:capn + 2, 0:domain_ref.shape[2]] = domain_ref[0]
    tab[capn + 2:capn + 3, 0:ghost_ref.shape[1]] = ghost_ref[...]
    greet(n_dom, n_node)
    parts = ((pos_ref, recv_ref), (mass_ref, rmass_ref), (tab, rtab_ref))

    def copies(lane, target, slot):
        return [
            pltpu.make_async_remote_copy(
                src_ref=src,
                dst_ref=dst.at[slot],
                send_sem=send.at[lane, part],
                recv_sem=land.at[lane, part],
                device_id=target,
                device_id_type=MESH,
            )
            for part, (src, dst) in enumerate(parts)
        ]

    def blanks(lane, slot):
        return [
            pltpu.make_async_copy(none, recv_ref.at[slot], local.at[lane, 0]),
            pltpu.make_async_copy(none.at[0:1], rmass_ref.at[slot], local.at[lane, 1]),
            pltpu.make_async_copy(no_tab, rtab_ref.at[slot], local.at[lane, 2]),
        ]

    to_prev = copies(0, (a - 1, c), next_slot)
    to_next = copies(1, (a + 1, c), prev_slot)
    around = [
        copies(1 + turn, (a, lax.rem(c + turn, n_node)), c) for turn in range(1, n_node)
    ]
    own = [
        pltpu.make_async_copy(src, dst.at[c], local.at[0, part])
        for part, (src, dst) in enumerate(parts)
    ]
    finish(a, n_dom, to_prev, to_next, around, own, blanks(1, prev_slot), blanks(2, next_slot))


def finish(a, n_dom, to_prev, to_next, around, own, prev_blank, next_blank):
    def each(copies, act):
        for copy in copies:
            getattr(copy, act)()

    @pl.when(a > 0)
    def _():
        for copy in to_prev:
            copy.start()

    @pl.when(a < n_dom - 1)
    def _():
        for copy in to_next:
            copy.start()

    for group in around:
        each(group, "start")
    each(own, "start")

    @pl.when(a == 0)
    def _():
        each(prev_blank, "start")
        each(prev_blank, "wait")

    @pl.when(a == n_dom - 1)
    def _():
        each(next_blank, "start")
        each(next_blank, "wait")

    each(own, "wait")
    for group in around:
        each(group, "wait")

    @pl.when(a > 0)
    def _():
        for copy in to_prev:
            copy.wait_send()
        for copy in to_next:
            copy.wait_recv()

    @pl.when(a < n_dom - 1)
    def _():
        for copy in to_next:
            copy.wait_send()
        for copy in to_prev:
            copy.wait_recv()


def term_exchange(n_dom, n_node, capn, capd, pay_ref, recv_ref, send, land, local):
    a, c = lax.axis_index("dom"), lax.axis_index("node")
    first = n_node * capn
    prev_cols = pl.ds(first * SIZE, capd * SIZE)
    next_cols = pl.ds((first + capd) * SIZE, capd * SIZE)
    greet(n_dom, n_node)

    def copies(lane, target, src, dst):
        return [
            pltpu.make_async_remote_copy(
                src_ref=pay_ref.at[:, src],
                dst_ref=recv_ref.at[:, dst],
                send_sem=send.at[lane],
                recv_sem=land.at[lane],
                device_id=target,
                device_id_type=MESH,
            )
        ]

    to_prev = copies(0, (a - 1, c), prev_cols, next_cols)
    to_next = copies(1, (a + 1, c), next_cols, prev_cols)
    around = []
    for turn in range(1, n_node):
        peer = lax.rem(c + turn, n_node)
        around.append(copies(1 + turn, (a, peer), lanes(peer * capn, capn), lanes(c * capn, capn)))

    def kept(lane, cols):
        return [pltpu.make_async_copy(pay_ref.at[:, cols], recv_ref.at[:, cols], local.at[lane])]

    own = kept(0, lanes(c * capn, capn))
    finish(a, n_dom, to_prev, to_next, around, own, kept(1, prev_cols), kept(2, next_cols))


def set_parts(out, base, values, order):
    count = values[0].shape[0]
    for k, value in enumerate(values):
        high = value.astype(BF16).astype(F32)
        rest = value - high
        middle = rest.astype(BF16).astype(F32)
        parts = (high, middle, rest - middle)
        for group, part in enumerate(order):
            at = base + (TERMS * group + k) * count
            out[at:at + count, :] = parts[part]


def split2(value):
    high = value.astype(BF16)
    return high, (value - high.astype(F32)).astype(BF16)


def dot(left, right):
    return jnp.dot(left, right, preferred_element_type=F32)


def inverse_parts(m):
    cofactors = [
        m[1] * m[2] - m[5] * m[5],
        m[0] * m[2] - m[4] * m[4],
        m[0] * m[1] - m[3] * m[3],
        m[4] * m[5] - m[3] * m[2],
        m[3] * m[5] - m[4] * m[1],
        m[3] * m[4] - m[0] * m[5],
    ]
    return cofactors, m[0] * cofactors[0] + m[3] * cofactors[3] + m[4] * cofactors[4]


def apply_metric(m, x):
    return [
        m[0] * x[0] + m[3] * x[1] + m[4] * x[2],
        m[3] * x[0] + m[1] * x[1] + m[5] * x[2],
        m[4] * x[0] + m[5] * x[1] + m[2] * x[2],
    ]


def inverse_of(s):
    return pltpu.reciprocal(s, approx=True)


def compute(
    n_dom, sizes,
    tab_ref, local_ref, recv_ref, rmass_ref, metric_ref, energy_ref,
    final_ref, density_ref, accel_ref, pay_ref,
    held, src, pack, low_t, high_t, twin_t, feat_m, narrow, coef, acc, thirds_acc, cubes, back_feat, backs, own,
):
    n_node, capn, capd, blocks = sizes
    ghosts = blocks * KG
    sources = blocks + 2 * ghosts
    first = n_node * capn
    ghost_row = capn + 2
    slots = n_node + 2
    c = lax.axis_index("node")

    def strided(n, count, stride):
        return pl.ds(n, count, stride=stride)

    def put_source(n, slot, at):
        src[strided(n, 3, sources), :] = recv_ref[slot, :, at]
        src[3 * sources + n:3 * sources + n + 1, :] = rmass_ref[slot, :, at]

    for slot in range(slots):
        if slot >= n_node:
            @pl.loop(0, ghosts, unroll=8)
            def _(n, slot=slot):
                held[slot, n] = 0

        @pl.loop(0, ghosts, unroll=8)
        def _(n, slot=slot):
            held[slot, tab_ref[slot, ghost_row, n]] = n // KG

    for n in range(blocks):
        at = slice(n * SIZE, (n + 1) * SIZE)
        put_source(n, c, at)
        own[strided(n, 6, blocks), :] = metric_ref[:, at]
        own[6 * blocks + n:6 * blocks + n + 1, :] = energy_ref[:, at]

    for n in range(ghosts):
        slot = tab_ref[c, ghost_row, n]
        near = slot < first
        low = slot < first + capd
        past = slot - first
        from_slot = jnp.where(near, slot // capn, jnp.where(low, n_node, n_node + 1))
        row = jnp.where(near, slot % capn, jnp.where(low, capn + 1, capn))
        col = jnp.where(near, c, jnp.where(low, past, past - capd))
        block = tab_ref[from_slot, row, col]
        put_source(blocks + n, from_slot, lanes(block))

    for n in range(ghosts):
        if n < first:
            from_slot, there = n // capn, c * capn + n % capn
        elif n < first + capd:
            from_slot, there = n_node, n + capd
        else:
            from_slot, there = n_node + 1, n - capd
        block = held[from_slot, there]
        put_source(blocks + ghosts + n, from_slot, lanes(block))

    def send_target(n):
        near = n < first
        low = n < first + capd
        past = n - first
        row = jnp.where(near, n % capn, jnp.where(low, capn, capn + 1))
        return tab_ref[c, row, jnp.where(near, n // capn, jnp.where(low, past, past - capd))]

    x, y, z, mass = (src[k * sources:(k + 1) * sources, :] for k in range(4))
    feature = [jnp.ones_like(x), x, y, z, x * x, y * y, z * z, x * y, x * z, y * z]
    pack[60 * sources:, :] = jnp.zeros((4 * sources, SIZE), F32)
    set_parts(pack, 0, feature, (0, 1, 0, 2, 1, 0))
    blank = jnp.zeros((HALF, SIZE), BF16)

    @pl.loop(0, blocks, unroll=4)
    def _(n):
        one = pack[strided(n, HALF, sources), :].astype(BF16)
        low_t[n] = jnp.concatenate([one, blank], axis=0).T
        high_t[n] = jnp.concatenate([blank, one], axis=0).T

    @pl.loop(0, ghosts, unroll=4)
    def _(n):
        one = pack[strided(blocks + 2 * n, HALF, sources), :].astype(BF16)
        other = pack[strided(blocks + 2 * n + 1, HALF, sources), :].astype(BF16)
        twin_t[n] = jnp.concatenate([one, other], axis=0).T

    pack[30 * sources:32 * sources, :] = jnp.zeros((2 * sources, SIZE), F32)
    set_parts(pack, 0, [row * mass for row in feature], (0, 1, 2))

    @pl.loop(0, sources, unroll=8)
    def _(n):
        feat_m[n] = pack[strided(n, 32, sources), :].astype(BF16)

    def set_coefficients(g, r):
        gr = apply_metric(g, r)
        rows = [
            1.0 + gr[0] * r[0] + gr[1] * r[1] + gr[2] * r[2],
            -2.0 * gr[0], -2.0 * gr[1], -2.0 * gr[2],
            g[0], g[1], g[2], 2.0 * g[3], 2.0 * g[4], 2.0 * g[5],
        ]
        set_parts(narrow, 0, rows, (0, 0, 1, 0, 1, 2))
        for t in range(blocks):
            coef[t] = narrow[strided(t, HALF, blocks), :].astype(BF16)

    def units(e):
        local = local_ref[0, e]
        sent = [send_target(KG * e + k) for k in range(KG)]
        ghost, back = blocks + KG * e, blocks + ghosts + KG * e
        return [
            ((e, ghost), (e, ghost + 1)),
            ((sent[0], back), (sent[1], back + 1)),
            ((e, local), (local, e)),
        ]

    def quads(e, kind, unit):
        if kind == 0:
            left = twin_t[e]
        elif kind == 1:
            left = twin_t[blocks + e]
        else:
            left = low_t[unit[0][1]] + high_t[unit[1][1]]
        none = jnp.zeros((HALF, SIZE), BF16)
        top = jnp.concatenate([coef[unit[0][0]], none], axis=1)
        bottom = jnp.concatenate([none, coef[unit[1][0]]], axis=1)
        return dot(left, jnp.concatenate([top, bottom], axis=0))

    def mass_rows(unit):
        one, other = (feat_m[source] for _, source in unit)
        return jnp.concatenate(
            [jnp.concatenate([one, one], axis=1), jnp.concatenate([other, other], axis=1)], axis=0
        )

    def stacked(value):
        return jnp.concatenate(split2(value), axis=0)

    def listed_units(e):
        return [
            (e + step, kind, unit)
            for step in range(STEPS)
            for kind, unit in enumerate(units(e + step))
        ]

    def ahead(listed):
        waiting = []
        for index, item in enumerate(listed):
            waiting.append(quads(*item))
            if index >= AHEAD:
                yield index - AHEAD, listed[index - AHEAD], inverse_of(waiting[index - AHEAD])
        for index in range(max(len(listed) - AHEAD, 0), len(listed)):
            yield index, listed[index], inverse_of(waiting[index])

    def rows_of(block):
        return pl.ds(pl.multiple_of(block * 32, 32), 32)

    def add_sums(into, listed, sums):
        for (e, kind, unit), value in zip(listed, sums):
            one, other = value[0:32, 0:SIZE], value[32:64, SIZE:2 * SIZE]
            if kind == 0:
                into[rows_of(e), :] += one + other
            else:
                into[rows_of(unit[0][0]), :] += one
                into[rows_of(unit[1][0]), :] += other

    def summed(ref, k, count):
        low, middle, high = (ref[strided(k + TERMS * part, count, 32), :] for part in (2, 1, 0))
        return high + (middle + low)

    def place():
        return [src[k * sources:k * sources + blocks, :] for k in range(3)]

    def metric():
        return [own[k * blocks:(k + 1) * blocks, :] for k in range(6)]

    narrow[60 * blocks:, :] = jnp.zeros((4 * blocks, SIZE), F32)

    @pl.loop(0, ITERS)
    def _(iteration):
        g, r = metric(), place()
        set_coefficients(g, r)
        acc[...] = jnp.zeros(acc.shape, F32)

        @pl.loop(0, blocks, step=STEPS)
        def _(e):
            listed = listed_units(e)
            sums = []
            for _, (_, _, unit), inv in ahead(listed):
                sums.append(dot(mass_rows(unit), stacked(inv * inv)))
            add_sums(acc, listed, sums)

        s = [summed(acc, k, blocks) for k in range(TERMS)]
        g, r = metric(), place()
        total = s[0]
        share = 1.0 / total

        def second(i, j, at):
            return (r[i] * r[j] * total - r[i] * s[1 + j] - r[j] * s[1 + i] + s[at]) * share

        spread = [
            second(0, 0, 4) + RIDGE_TERM,
            second(1, 1, 5) + RIDGE_TERM,
            second(2, 2, 6) + RIDGE_TERM,
            second(0, 1, 7),
            second(0, 2, 8),
            second(1, 2, 9),
        ]
        cofactors, determinant = inverse_parts(spread)
        weight = 0.5 * TARGET_SCALE / determinant
        for k in range(6):
            own[k * blocks:(k + 1) * blocks, :] = 0.5 * g[k] + cofactors[k] * weight

    set_coefficients(metric(), place())
    acc[...] = jnp.zeros(acc.shape, F32)
    thirds_acc[...] = jnp.zeros(thirds_acc.shape, F32)

    @pl.loop(0, blocks, step=STEPS)
    def _(e):
        listed = listed_units(e)
        squares, thirds = [], []
        for index, (_, _, unit), inv in ahead(listed):
            square = inv * inv
            cube = stacked(square * inv)
            cubes[3 * e + index] = cube
            left = mass_rows(unit)
            squares.append(dot(left, stacked(square)))
            thirds.append(dot(left, cube))
        add_sums(acc, listed, squares)
        add_sums(thirds_acc, listed, thirds)

    g, r = metric(), place()
    cofactors, determinant = inverse_parts(g)
    volume = jnp.sqrt(determinant) / (SIZE * LISTED)
    density = volume * summed(acc, 0, blocks)
    energy = own[6 * blocks:7 * blocks, :]
    coefficient = (ADIABATIC - 1.0) * energy / density * volume
    scale = 4.0 * src[3 * sources:3 * sources + blocks, :] * coefficient
    own[6 * blocks:7 * blocks, :] = density
    own[7 * blocks:8 * blocks, :] = coefficient
    set_parts(narrow, 0, [scale * row for row in g + apply_metric(g, r) + [jnp.zeros_like(scale)]], (0, 1, 2))
    narrow[30 * blocks:32 * blocks, :] = jnp.zeros((2 * blocks, SIZE), F32)
    for t in range(blocks):
        back_feat[t] = narrow[strided(t, 32, blocks), :].astype(BF16)
    backs[0:32 * blocks, :] = jnp.zeros((32 * blocks, SIZE), F32)

    @pl.loop(0, blocks, step=STEPS)
    def _(e):
        listed = listed_units(e)
        values = []
        for index, (at, kind, unit) in enumerate(listed):
            one, other = (back_feat[target] for target, _ in unit)
            none = jnp.zeros((32, SIZE), BF16)
            left = jnp.concatenate(
                [jnp.concatenate([one, none], axis=1), jnp.concatenate([none, other], axis=1)], axis=0
            )
            value = lax.dot_general(
                left, cubes[3 * e + index], (((1,), (1,)), ((), ())), preferred_element_type=F32
            )
            values.append(value[:, 0:SIZE] + value[:, SIZE:2 * SIZE])
        for (_, kind, unit), value in zip(listed, values):
            for half, (_, source) in enumerate(unit):
                if kind < 2:
                    backs[rows_of(source), :] = value[32 * half:32 * half + 32]
        for (_, kind, unit), value in zip(listed, values):
            for half, (_, source) in enumerate(unit):
                if kind == 2:
                    backs[rows_of(source), :] += value[32 * half:32 * half + 32]

    b = [summed(backs, k, sources) for k in range(9)]
    where = [src[k * sources:(k + 1) * sources, :] for k in range(3)]
    back = [moved - b[6 + k] for k, moved in enumerate(apply_metric(b[0:6], where))]
    f = [summed(thirds_acc, k, blocks) for k in range(4)]
    g, r = metric(), place()
    coefficient = own[7 * blocks:8 * blocks, :]
    forward = apply_metric(g, [r[k] * f[0] - f[1 + k] for k in range(3)])
    for k in range(3):
        pack[k * sources:(k + 1) * sources, :] = back[k]
        narrow[k * blocks:(k + 1) * blocks, :] = 4.0 * coefficient * forward[k] + back[k][0:blocks]
    for t in range(blocks):
        at = slice(t * SIZE, (t + 1) * SIZE)
        final_ref[:, at] = own[strided(t, 6, blocks), :]
        density_ref[:, at] = own[6 * blocks + t:6 * blocks + t + 1, :]
        accel_ref[:, at] = narrow[strided(t, 3, blocks), :]

    for n in range(ghosts):
        pay_ref[4:7, n * SIZE:(n + 1) * SIZE] = pack[strided(blocks + ghosts + n, 3, sources), :]
        slot = tab_ref[c, ghost_row, n]
        pay_ref[0:3, lanes(slot)] = pack[strided(blocks + n, 3, sources), :]

    a = lax.axis_index("dom")

    @pl.when(a == 0)
    def _():
        pay_ref[:, first * SIZE:(first + capd) * SIZE] = jnp.zeros((8, capd * SIZE), F32)

    @pl.when(a == n_dom - 1)
    def _():
        pay_ref[:, (first + capd) * SIZE:ghosts * SIZE] = jnp.zeros((8, capd * SIZE), F32)


def add_terms(sizes, tab_ref, part_ref, recv_ref, out_ref):
    n_node, capn, capd, blocks = sizes
    c = lax.axis_index("node")
    out_ref[...] = part_ref[...]
    for n in range(blocks * KG):
        past = n - n_node * capn
        row, col = (n % capn, n // capn) if past < 0 else (capn + past // capd, past % capd)
        at = slice(n * SIZE, (n + 1) * SIZE)
        out_ref[:, lanes(tab_ref[c, row, col])] += recv_ref[0:3, at]
    for e in range(blocks):
        at = slice(e * SIZE, (e + 1) * SIZE)
        terms = [recv_ref[4:7, lanes(tab_ref[c, capn + 2, KG * e + k])] for k in range(KG)]
        out_ref[:, at] += sum(terms[1:], terms[0])


def on_device(n_dom, n_node, positions, masses, metric, energy, local_pairs, ghost_pairs, node_sends, domain_sends):
    blocks = local_pairs.shape[0]
    capn, capd = node_sends.shape[2], domain_sends.shape[2]
    ghosts = blocks * KG
    width = blocks * SIZE
    sources = blocks + 2 * ghosts
    slots = n_node + 2
    sizes = (n_node, capn, capd, blocks)
    rows = -(-(capn + 3) // 8) * 8
    vmem = pl.BlockSpec(memory_space=pltpu.VMEM)
    smem = pl.BlockSpec(memory_space=pltpu.SMEM)
    anywhere = pl.BlockSpec(memory_space=pl.ANY)
    received, rmass, tables = pl.pallas_call(
        functools.partial(static_exchange, n_dom, n_node),
        out_shape=(
            jax.ShapeDtypeStruct((slots, 3, width), F32),
            jax.ShapeDtypeStruct((slots, 1, width), F32),
            jax.ShapeDtypeStruct((slots, rows, SIZE), jnp.int32),
        ),
        in_specs=[anywhere] * 2 + [vmem] * 3,
        out_specs=(anywhere,) * 3,
        scratch_shapes=[
            pltpu.VMEM((rows, SIZE), jnp.int32),
            pltpu.VMEM((3, width), F32),
            pltpu.VMEM((rows, SIZE), jnp.int32),
            pltpu.SemaphoreType.DMA((n_node + 1, 3)),
            pltpu.SemaphoreType.DMA((n_node + 1, 3)),
            pltpu.SemaphoreType.DMA((3, 3)),
        ],
        compiler_params=pltpu.CompilerParams(collective_id=0, has_side_effects=True),
        name="static_exchange",
    )(positions, masses.reshape(1, width), node_sends.swapaxes(1, 2), domain_sends, ghost_pairs)
    final, density, part, pay = pl.pallas_call(
        functools.partial(compute, n_dom, sizes),
        out_shape=(
            jax.ShapeDtypeStruct((6, width), F32),
            jax.ShapeDtypeStruct((1, width), F32),
            jax.ShapeDtypeStruct((3, width), F32),
            jax.ShapeDtypeStruct((8, ghosts * SIZE), F32),
        ),
        in_specs=[smem, smem, vmem, vmem, vmem, vmem],
        out_specs=(vmem,) * 4,
        scratch_shapes=[
            pltpu.SMEM((slots, ghosts), jnp.int32),
            pltpu.VMEM((4 * sources, SIZE), F32),
            pltpu.VMEM((HALF * sources, SIZE), F32),
            pltpu.VMEM((blocks, SIZE, SIZE), BF16),
            pltpu.VMEM((blocks, SIZE, SIZE), BF16),
            pltpu.VMEM((ghosts, SIZE, SIZE), BF16),
            pltpu.VMEM((sources, 32, SIZE), BF16),
            pltpu.VMEM((HALF * blocks, SIZE), F32),
            pltpu.VMEM((blocks, HALF, SIZE), BF16),
            pltpu.VMEM((32 * blocks, SIZE), F32),
            pltpu.VMEM((32 * blocks, SIZE), F32),
            pltpu.VMEM((3 * blocks, 2 * SIZE, 2 * SIZE), BF16),
            pltpu.VMEM((blocks, 32, SIZE), BF16),
            pltpu.VMEM((32 * sources, SIZE), F32),
            pltpu.VMEM((8 * blocks, SIZE), F32),
        ],
        compiler_params=pltpu.CompilerParams(vmem_limit_bytes=62 * 2**20),
        name="compute",
    )(tables, local_pairs.T, received, rmass, metric, energy.reshape(1, width))
    returned = pl.pallas_call(
        functools.partial(term_exchange, n_dom, n_node, capn, capd),
        out_shape=jax.ShapeDtypeStruct((8, ghosts * SIZE), F32),
        in_specs=[anywhere],
        out_specs=anywhere,
        scratch_shapes=[
            pltpu.SemaphoreType.DMA((n_node + 1,)),
            pltpu.SemaphoreType.DMA((n_node + 1,)),
            pltpu.SemaphoreType.DMA((3,)),
        ],
        compiler_params=pltpu.CompilerParams(collective_id=1, has_side_effects=True),
        name="term_exchange",
    )(pay)
    accel = pl.pallas_call(
        functools.partial(add_terms, sizes),
        out_shape=jax.ShapeDtypeStruct((3, width), F32),
        in_specs=[smem, vmem, vmem],
        out_specs=vmem,
        name="add_terms",
    )(tables, part, returned)
    return (final, density.reshape(-1), accel)


def solution(mesh):
    in_specs = (
        P(None, ("dom", "node")),
        P(("dom", "node")),
        P(None, ("dom", "node")),
        P(("dom", "node")),
        P(("dom", "node"), None),
        P(("dom", "node"), None),
        P(("dom", "node"), None, None),
        P(("dom", "node"), None, None),
    )
    out_specs = (P(None, ("dom", "node")), P(("dom", "node")), P(None, ("dom", "node")))
    return jax.shard_map(
        functools.partial(on_device, mesh.shape["dom"], mesh.shape["node"]),
        mesh=mesh, in_specs=in_specs, out_specs=out_specs, check_vma=False,
    )
```
